32 devices in a mesh: runs: 2 (over y), gy: 4 (over z), gx: 2 (over x), gz: 2 (over core).
Axes of the slice: x: 2, y: 2, z: 4, core: 2. Of those that a mesh axis runs over, the one named last changes fastest.
Arguments:
- box_state: float32 [8, 4, 2048, 256], P(None, 'gx', ('runs', 'gy'), 'gz'), parts along dimension 2, may hold values from -6 to 6
- shear_cells: int32 [4], P('runs'), parts along dimension 0, may hold values from 0 to 1023
- shear_fraction: float32 [4], P('runs'), parts along dimension 0, may hold values from 0 to 1
Outputs:
- advanced: float32 [8, 4, 2048, 256], P(None, 'gx', ('runs', 'gy'), 'gz'), parts along dimension 2
The draws below stay inside these ranges and needn't reach their ends.
There are 2 independent parts, one for each index of `runs`. The reference program is written for one: setup_inputs(seed, part) draws one part's arguments, and reference() takes and returns one part's arrays. A program takes and returns all parts, laid end to end along the dimension named above; each array names one. Nothing has to cross between parts.
Inputs may be any that keep to these rules, and one draw needn't show every extreme that they name: `shear_cells`: whole cells of each section's azimuthal shear offset.
All inputs are finite; a program needn't handle non-finite values.
Results may differ from the reference program's by a relative error of at most 0.0003.
Values sent between devices are 32-bit elements; how exact they have to be, the bound alone decides.
A program may use at most 128 MiB of HBM per device.

```python
import math
import jax
import jax.numpy as jnp
from jax import lax

F = 8
GHOST = 2
SECTIONS = 2
NY = 1024
NX = 4
NZ = 256


def block_scale(rng, dims, cuts, least, high):
    factor_of, own = 1.0, jax.random.fold_in(rng, 6)
    for dim, parts in cuts:
        steps = jnp.exp(jax.random.uniform(jax.random.fold_in(own, dim), (parts,), jnp.float32, least / len(cuts), high / len(cuts)))
        factor_of = factor_of * jnp.repeat(steps, dims[dim] // parts).reshape([-1 if axis == dim else 1 for axis in range(len(dims))])
    return factor_of


def gaussian(rng, shape, scale, most, cuts=(), held_as=jnp.bfloat16):
    gain = block_scale(rng, shape, cuts, -0.22, 0.18) if cuts else 1.0
    drawn = jax.random.normal(rng, shape, jnp.float32) * scale * gain
    return jnp.minimum(jnp.maximum(drawn, -most), most).astype(held_as)


def setup_inputs(seed: int = 0, part: int = 0) -> dict:
    streams_of = jax.random.split(jax.random.key(seed), 4)
    own_keys = jax.random.split(jax.random.fold_in(streams_of[3], part), 4)
    return {
        "box_state": gaussian(own_keys[0], (F, NX, NY, NZ), 1.0, 6.0, ((1, 2), (2, 4), (3, 2)), jnp.float32),
        "shear_cells": jax.random.randint(own_keys[1], (SECTIONS,), 0, NY).astype(jnp.int32),
        "shear_fraction": jnp.clip(jax.random.uniform(own_keys[2], (SECTIONS,), jnp.float32, 0.0, 1.0), 0.0, 1.0),
    }


time_step = 0.25
sound_sq = 1.0
guide_field = 0.8
rotation = 1.0
shear_rate = 1.5
viscosity = 0.15
resistivity = 0.15
clean_sq = 1.0
damping_time = 2.0


def shifted_slice(padded, start, dimension):
    length = padded.shape[dimension] - 4
    return lax.slice_in_dim(padded, start, start + length, axis=dimension)


def first_difference(padded, dimension):
    return (8.0 * (shifted_slice(padded, 3, dimension) - shifted_slice(padded, 1, dimension))
            - (shifted_slice(padded, 4, dimension) - shifted_slice(padded, 0, dimension))) / 12.0


def second_difference(padded, dimension):
    return (16.0 * (shifted_slice(padded, 3, dimension) + shifted_slice(padded, 1, dimension))
            - (shifted_slice(padded, 4, dimension) + shifted_slice(padded, 0, dimension))
            - 30.0 * shifted_slice(padded, 2, dimension)) / 12.0


def tendency(fields, derivative, laplace):
    velocity_div = derivative(1, 0) + derivative(2, 1) + derivative(3, 2)
    return [
        -velocity_div,
        -sound_sq * derivative(0, 0) + guide_field * (derivative(4, 2) - derivative(6, 0)) + 2.0 * rotation * fields[2] + viscosity * laplace(1),
        -sound_sq * derivative(0, 1) + guide_field * (derivative(5, 2) - derivative(6, 1)) - (2.0 - shear_rate) * rotation * fields[1] + viscosity * laplace(2),
        -sound_sq * derivative(0, 2) + viscosity * laplace(3),
        guide_field * derivative(1, 2) - derivative(7, 0) + resistivity * laplace(4),
        guide_field * derivative(2, 2) - shear_rate * rotation * fields[4] - derivative(7, 1) + resistivity * laplace(5),
        -guide_field * (derivative(1, 0) + derivative(2, 1)) - derivative(7, 2) + resistivity * laplace(6),
        -clean_sq * (derivative(4, 0) + derivative(5, 1) + derivative(6, 2)) - fields[7] / damping_time,
    ]


def shear_remap(strip_cells, whole_cells, fraction, direction):
    length = strip_cells.shape[2]
    frequency = jnp.arange(length, dtype=jnp.int32)
    signed = jnp.where(frequency <= length // 2, frequency, frequency - length).astype(jnp.int32)
    turn_count = jnp.mod(signed * whole_cells, length).astype(jnp.float32) + signed.astype(jnp.float32) * fraction
    phase_angle = (direction * 2.0 * math.pi / length) * turn_count
    spectrum = jnp.fft.fft(strip_cells, axis=2)
    rotated = spectrum * (jnp.cos(phase_angle) + 1j * jnp.sin(phase_angle))[None, None, :, None]
    return jnp.real(jnp.fft.ifft(rotated, axis=2)).astype(jnp.float32)


def padded_field(field_cells, ghost_left, ghost_right, dimension):
    if dimension == 0:
        return jnp.concatenate([ghost_left, field_cells, ghost_right], axis=0)
    widths = [(0, 0), (0, 0), (0, 0)]
    widths[dimension] = (GHOST, GHOST)
    return jnp.pad(field_cells, widths, mode="wrap")


def section_rates(current, whole_cells, fraction):
    radial = current.shape[1]
    left_side = shear_remap(current[:, radial - GHOST:], whole_cells, fraction, 1.0)
    right_side = shear_remap(current[:, :GHOST], whole_cells, fraction, -1.0)

    def derivative(field_index, dimension):
        return first_difference(padded_field(current[field_index], left_side[field_index], right_side[field_index], dimension), dimension)

    def laplace(field_index):
        total = second_difference(padded_field(current[field_index], left_side[field_index], right_side[field_index], 0), 0)
        total = total + second_difference(padded_field(current[field_index], left_side[field_index], right_side[field_index], 1), 1)
        return total + second_difference(padded_field(current[field_index], left_side[field_index], right_side[field_index], 2), 2)

    return jnp.stack(tendency(current, derivative, laplace))


def reference(box_state, shear_cells, shear_fraction):
    rate_one = section_rates(box_state, shear_cells[0], shear_fraction[0])
    section_one = box_state + time_step * rate_one
    rate_two = section_rates(section_one, shear_cells[1], shear_fraction[1])
    return 0.5 * box_state + 0.5 * (section_one + time_step * rate_two)
```

```python
import math

import jax
import jax.numpy as jnp
from jax import lax
from jax.sharding import PartitionSpec as P

GHOST = 2

time_step = 0.25
sound_sq = 1.0
guide_field = 0.8
rotation = 1.0
shear_rate = 1.5
viscosity = 0.15
resistivity = 0.15
clean_sq = 1.0
damping_time = 2.0


def circulant(length, whole_cells, fraction, sign):
    rows = math.gcd(length, 128)
    j = lax.broadcasted_iota(jnp.int32, (rows, length), 1)
    m = lax.broadcasted_iota(jnp.int32, (rows, length), 0)
    q = jnp.mod(j - m + sign * whole_cells + length // 2, length) - length // 2
    x = q.astype(jnp.float32) + sign.astype(jnp.float32) * fraction
    parity = (1 - 2 * jnp.bitwise_and(q, 1)).astype(jnp.float32) * sign.astype(jnp.float32)
    sine = jnp.sin(math.pi * jnp.minimum(fraction, 1.0 - fraction))
    angle = (math.pi / length) * x
    near = jnp.abs(x) < 1e-5
    h = parity * (sine / length) * jnp.cos(angle) / jnp.where(near, 1.0, jnp.sin(angle))
    block = jnp.where(near, 1.0, h)
    return jnp.concatenate(
        [jnp.roll(block, rows * b, axis=1) for b in range(length // rows)], axis=0
    )


def remap(cells, matrix):
    return lax.dot_general(
        cells,
        matrix,
        (((cells.ndim - 1,), (0,)), ((), ())),
        precision=lax.Precision.HIGH,
        preferred_element_type=jnp.float32,
    )


def rates(left, cells, right):
    radial, vertical = cells.shape[1], cells.shape[2] - 2 * GHOST
    inner = cells[:, :, GHOST:-GHOST]
    padded = jnp.concatenate([left, inner, right], axis=1)

    def at(f, dim, step):
        if dim == 0:
            return padded[f, GHOST + step : GHOST + step + radial]
        if dim == 2:
            return cells[f, :, GHOST + step : GHOST + step + vertical]
        return jnp.roll(inner[f], -step, axis=-1)

    def d(f, dim):
        return (8.0 * (at(f, dim, 1) - at(f, dim, -1)) - (at(f, dim, 2) - at(f, dim, -2))) / 12.0

    def second(f, dim):
        return (
            16.0 * (at(f, dim, 1) + at(f, dim, -1))
            - (at(f, dim, 2) + at(f, dim, -2))
            - 30.0 * inner[f]
        ) / 12.0

    def lap(f):
        return second(f, 0) + second(f, 1) + second(f, 2)

    return jnp.stack([
        -(d(1, 0) + d(2, 1) + d(3, 2)),
        -sound_sq * d(0, 0) + guide_field * (d(4, 2) - d(6, 0)) + 2.0 * rotation * inner[2] + viscosity * lap(1),
        -sound_sq * d(0, 1) + guide_field * (d(5, 2) - d(6, 1)) - (2.0 - shear_rate) * rotation * inner[1] + viscosity * lap(2),
        -sound_sq * d(0, 2) + viscosity * lap(3),
        guide_field * d(1, 2) - d(7, 0) + resistivity * lap(4),
        guide_field * d(2, 2) - shear_rate * rotation * inner[4] - d(7, 1) + resistivity * lap(5),
        -guide_field * (d(1, 0) + d(2, 1)) - d(7, 2) + resistivity * lap(6),
        -clean_sq * (d(4, 0) + d(5, 1) + d(6, 2)) - inner[7] / damping_time,
    ])


def around(x, axis, width, dim):
    devices, length = lax.axis_size(axis), x.shape[dim]
    up = [(i, (i + 1) % devices) for i in range(devices)]
    down = [(j, i) for i, j in up]
    before = lax.ppermute(lax.slice_in_dim(x, length - width, length, axis=dim), axis, up)
    after = lax.ppermute(lax.slice_in_dim(x, 0, width, axis=dim), axis, down)
    return before, after


def body(box_state, shear_cells, shear_fraction):
    fields, radial, azimuth, vertical = box_state.shape
    gx, gy = lax.axis_size("gx"), lax.axis_size("gy")
    length, part, wide = gy * azimuth, vertical // gy, 2 * GHOST
    at_left = lax.axis_index("gx") == 0
    at_right = lax.axis_index("gx") == gx - 1
    plus, minus = jnp.int32(1), jnp.int32(-1)

    turned = jnp.transpose(box_state, (0, 1, 3, 2))
    before, after = around(turned, "gz", wide, 2)
    turned = jnp.concatenate([before, turned, after], axis=2)
    chunks = jnp.stack([turned[:, :, part * i : part * (i + 1) + 2 * wide] for i in range(gy)])
    spread = lax.all_to_all(chunks, "gy", split_axis=0, concat_axis=0)
    own = jnp.concatenate([spread[i] for i in range(gy)], axis=-1)

    sign = jnp.where(at_left, plus, minus)
    edge = circulant(length, shear_cells[1], shear_fraction[1], sign)

    def cut(x, width):
        return x[:, :, width:-width]

    if gx == 2 and radial == 2:
        other = lax.ppermute(own, "gx", [(0, 1), (1, 0)])
        low = jnp.where(at_left, own, other)
        high = jnp.where(at_left, other, own)
        whole = jnp.concatenate([low, high], axis=1)
        raw = cut(whole, GHOST)
        left = remap(raw[:, 2:], circulant(length, shear_cells[0], shear_fraction[0], plus))
        right = remap(raw[:, :2], circulant(length, shear_cells[0], shear_fraction[0], minus))
        one = raw + time_step * rates(left, whole, right)
        one_low, one_high = one[:, :2], one[:, 2:]
        mine = jnp.where(at_left, one_low, one_high)
        raw_other = cut(jnp.where(at_left, one_high, one_low), GHOST)
        moved = remap(raw_other, edge)
        left = jnp.where(at_left, moved, raw_other)
        right = jnp.where(at_left, raw_other, moved)
    else:
        def sides(x, matrix):
            before, after = around(x, "gx", GHOST, 1)
            moved = remap(jnp.where(at_left, before, after), matrix)
            return jnp.where(at_left, moved, before), jnp.where(at_right, moved, after)

        first = circulant(length, shear_cells[0], shear_fraction[0], sign)
        raw = cut(own, GHOST)
        left, right = sides(raw, first)
        mine = raw + time_step * rates(left, own, right)
        left, right = sides(cut(mine, GHOST), edge)
    two = 0.5 * cut(own, wide) + 0.5 * (cut(mine, GHOST) + time_step * rates(left, mine, right))

    pieces = jnp.stack([two[..., azimuth * i : azimuth * (i + 1)] for i in range(gy)])
    back = lax.all_to_all(pieces, "gy", split_axis=0, concat_axis=0)
    joined = jnp.concatenate([back[i] for i in range(gy)], axis=2)
    return jnp.transpose(joined, (0, 1, 3, 2))


def solution(mesh):
    return jax.shard_map(
        body,
        mesh=mesh,
        in_specs=(P(None, "gx", ("runs", "gy"), "gz"), P("runs"), P("runs")),
        out_specs=P(None, "gx", ("runs", "gy"), "gz"),
        check_vma=False,
    )
```

```python
import functools
import math

import jax
import jax.numpy as jnp
from jax import lax
from jax.experimental import pallas as pl
from jax.experimental.pallas import tpu as pltpu
from jax.sharding import PartitionSpec as P

GHOST = 2

time_step = 0.25
sound_sq = 1.0
guide_field = 0.8
rotation = 1.0
shear_rate = 1.5
viscosity = 0.15
resistivity = 0.15
clean_sq = 1.0
damping_time = 2.0


MESH = pl.DeviceIdType.MESH
PAD = 8


def first_rows(rows, length, whole_cells, fraction, sign):
    j = lax.broadcasted_iota(jnp.int32, (rows, length), 1)
    m = lax.broadcasted_iota(jnp.int32, (rows, length), 0)
    q = jnp.mod(j - m + sign * whole_cells + length // 2, length) - length // 2
    x = q.astype(jnp.float32) + sign.astype(jnp.float32) * fraction
    parity = (1 - 2 * jnp.bitwise_and(q, 1)).astype(jnp.float32) * sign.astype(jnp.float32)
    sine = jnp.sin(math.pi * jnp.minimum(fraction, 1.0 - fraction))
    angle = (math.pi / length) * x
    near = jnp.abs(x) < 1e-5
    h = parity * (sine / length) * jnp.cos(angle) / jnp.where(near, 1.0, jnp.sin(angle))
    return jnp.where(near, 1.0, h)


def circulant(length, whole_cells, fraction, sign):
    rows = math.gcd(length, 128)
    block = first_rows(rows, length, whole_cells, fraction, sign)
    return jnp.concatenate(
        [jnp.roll(block, rows * b, axis=1) for b in range(length // rows)], axis=0
    )


def spread_kernel(gy, pieces, src, out, z_send, z_recv, x_send, x_recv, own_sem):
    me, x = lax.axis_index("gy"), lax.axis_index("gx")
    fields, radial, tall, azimuth = src.shape
    wide = out.shape[2]
    part = (tall - wide) // (gy - 1)
    group = fields // pieces
    others = [lax.rem(me + s, gy) for s in range(gy)]
    sources = [lax.rem(me - s + gy, gy) for s in range(gy)]

    barrier = pltpu.get_barrier_semaphore()
    for s in range(1, gy):
        pl.semaphore_signal(barrier, inc=1, device_id={"gy": others[s]}, device_id_type=MESH)
    pl.semaphore_signal(barrier, inc=1, device_id={"gx": 1 - x}, device_id_type=MESH)
    pl.semaphore_wait(barrier, gy)

    def taken(p, target):
        return src.at[pl.ds(p * group, group), :, pl.ds(pl.multiple_of(target * part, 8), wide), :]

    def place(p, source):
        return out.at[
            pl.ds(p * group, group),
            pl.ds(x * radial, radial),
            :,
            pl.ds(pl.multiple_of(source * azimuth, 128), azimuth),
        ]

    def over_z(p, s):
        return pltpu.make_async_remote_copy(
            src_ref=taken(p, others[s]), dst_ref=place(p, me),
            send_sem=z_send.at[p, s], recv_sem=z_recv.at[p, s],
            device_id={"gy": others[s]}, device_id_type=MESH,
        )

    def over_x(p, s):
        return pltpu.make_async_remote_copy(
            src_ref=taken(p, me) if s == 0 else place(p, sources[s]), dst_ref=place(p, sources[s]),
            send_sem=x_send.at[p, s], recv_sem=x_recv.at[p, s],
            device_id={"gx": 1 - x}, device_id_type=MESH,
        )

    def kept(p):
        return pltpu.make_async_copy(taken(p, me), place(p, me), own_sem.at[p])

    for p in range(pieces):
        over_x(p, 0).start()
        for s in range(1, gy):
            over_z(p, s).start()
    for p in range(pieces):
        kept(p).start()
    for p in range(pieces):
        for s in range(1, gy):
            over_z(p, s).wait_recv()
            over_x(p, s).start()
    for p in range(pieces):
        kept(p).wait()
        for s in range(1, gy):
            over_z(p, s).wait_send()

    for p in range(pieces):
        for s in range(gy):
            landed = pltpu.make_async_remote_copy(
                src_ref=taken(p, me),
                dst_ref=out.at[
                    pl.ds(p * group, group),
                    pl.ds((1 - x) * radial, radial),
                    :,
                    pl.ds(pl.multiple_of(sources[s] * azimuth, 128), azimuth),
                ],
                send_sem=x_send.at[p, s], recv_sem=x_recv.at[p, s],
                device_id={"gx": 1 - x}, device_id_type=MESH,
            )
            landed.wait_recv()
            over_x(p, s).wait_send()


def spread(turned, gy, wide):
    fields, radial, tall, azimuth = turned.shape
    pieces = 4
    return pl.pallas_call(
        functools.partial(spread_kernel, gy, pieces),
        out_shape=jax.ShapeDtypeStruct((fields, 2 * radial, wide, gy * azimuth), jnp.float32),
        in_specs=[pl.BlockSpec(memory_space=pl.ANY)],
        out_specs=pl.BlockSpec(memory_space=pl.ANY),
        scratch_shapes=[pltpu.SemaphoreType.DMA((pieces, gy))] * 4
        + [pltpu.SemaphoreType.DMA((pieces,))],
        compiler_params=pltpu.CompilerParams(collective_id=0, has_side_effects=True),
        name="spread",
    )(turned)


def gather_kernel(gy, src, out, send, recv, own_sem):
    me = lax.axis_index("gy")
    part, azimuth = src.shape[2], out.shape[3]
    others = [lax.rem(me + s, gy) for s in range(gy)]
    barrier = pltpu.get_barrier_semaphore()
    for s in range(1, gy):
        pl.semaphore_signal(barrier, inc=1, device_id={"gy": others[s]}, device_id_type=MESH)
    pl.semaphore_wait(barrier, gy - 1)

    def taken(target):
        return src.at[:, :, :, pl.ds(pl.multiple_of(target * azimuth, 128), azimuth)]

    place = out.at[:, :, pl.ds(pl.multiple_of(me * part, 8), part), :]
    copies = [
        pltpu.make_async_remote_copy(
            src_ref=taken(others[s]), dst_ref=place,
            send_sem=send.at[s], recv_sem=recv.at[s],
            device_id={"gy": others[s]}, device_id_type=MESH,
        )
        for s in range(1, gy)
    ]
    for copy in copies:
        copy.start()
    own = pltpu.make_async_copy(taken(me), place, own_sem)
    own.start()
    own.wait()
    for copy in copies:
        copy.wait()


def gather(two, gy):
    fields, radial, part, length = two.shape
    return pl.pallas_call(
        functools.partial(gather_kernel, gy),
        out_shape=jax.ShapeDtypeStruct((fields, radial, part * gy, length // gy), jnp.float32),
        in_specs=[pl.BlockSpec(memory_space=pl.ANY)],
        out_specs=pl.BlockSpec(memory_space=pl.ANY),
        scratch_shapes=[pltpu.SemaphoreType.DMA((gy,))] * 2 + [pltpu.SemaphoreType.DMA],
        compiler_params=pltpu.CompilerParams(collective_id=1, has_side_effects=True),
        name="gather",
    )(two)


def tile_rates(ref, r, row):
    length = ref.shape[3]

    def load(f, dr, dv):
        return ref[f, r + dr, pl.ds(row + dv, 8), :]

    centre, diff, one, two = [], [], [], []
    for f in range(8):
        c = load(f, 0, 0)
        near = [
            (load(f, 1, 0), load(f, -1, 0), load(f, 2, 0), load(f, -2, 0)),
            tuple(pltpu.roll(c, s % length, axis=1) for s in (-1, 1, -2, 2)),
            (load(f, 0, 1), load(f, 0, -1), load(f, 0, 2), load(f, 0, -2)),
        ]
        centre.append(c)
        diff.append([(2.0 / 3.0) * (n[0] - n[1]) - (1.0 / 12.0) * (n[2] - n[3]) for n in near])
        one.append(sum(n[0] + n[1] for n in near))
        two.append(sum(n[2] + n[3] for n in near))

    def d(f, dim):
        return diff[f][dim]

    def lap(f):
        return (4.0 / 3.0) * one[f] - (1.0 / 12.0) * two[f] - 7.5 * centre[f]

    flat = d(1, 0) + d(2, 1)
    return centre, [
        -(flat + d(3, 2)),
        -sound_sq * d(0, 0) + guide_field * (d(4, 2) - d(6, 0)) + 2.0 * rotation * centre[2] + viscosity * lap(1),
        -sound_sq * d(0, 1) + guide_field * (d(5, 2) - d(6, 1)) - (2.0 - shear_rate) * rotation * centre[1] + viscosity * lap(2),
        -sound_sq * d(0, 2) + viscosity * lap(3),
        guide_field * d(1, 2) - d(7, 0) + resistivity * lap(4),
        guide_field * d(2, 2) - shear_rate * rotation * centre[4] - d(7, 1) + resistivity * lap(5),
        -guide_field * flat - d(7, 2) + resistivity * lap(6),
        -clean_sq * (d(4, 0) + d(5, 1) + d(6, 2)) - (1.0 / damping_time) * centre[7],
    ]


def compute_kernel(side_ref, rows_ref, src, out, box, one, base, high, low, sem):
    fields, cells, wide, length = src.shape
    radial = cells // 2
    side = side_ref[0]
    copy = pltpu.make_async_copy(src, box.at[:, GHOST : GHOST + cells, PAD : PAD + wide, :], sem)
    copy.start()

    def build(i):
        block = base.shape[0]
        for a in range(block // 8):
            base[8 * a : 8 * a + 8, :] = pltpu.roll(rows_ref[i], 8 * a, axis=1) if a else rows_ref[i]
        whole = base[...]
        coarse = whole.astype(jnp.bfloat16)
        fine = (whole - coarse.astype(jnp.float32)).astype(jnp.bfloat16)
        for b in range(length // block):
            for part, ref in ((coarse, high), (fine, low)):
                cut = length - block * b
                turned = jnp.concatenate([part[:, cut:], part[:, :cut]], axis=1) if b else part
                ref[block * b : block * (b + 1), :] = turned

    def move(ref, source, target):
        count = 4

        def step(k, carry):
            f = k * count
            v = ref[pl.ds(f, count), pl.ds(source, GHOST), PAD : PAD + wide, :]
            v = v.reshape(count * GHOST * wide, length)
            coarse = v.astype(jnp.bfloat16)
            fine = (v - coarse.astype(jnp.float32)).astype(jnp.bfloat16)
            dot = functools.partial(jnp.dot, preferred_element_type=jnp.float32)
            moved = dot(coarse, high[...]) + dot(fine, high[...]) + dot(coarse, low[...])
            ref[pl.ds(f, count), pl.ds(target, GHOST), PAD : PAD + wide, :] = moved.reshape(
                count, GHOST, wide, length
            )
            return carry

        lax.fori_loop(0, fields // count, step, 0)

    build(0)

    def clear(f, carry):
        edge = jnp.zeros((cells + 2 * GHOST, PAD, length), jnp.float32)
        box[f, :, :PAD, :] = edge
        box[f, :, PAD + wide :, :] = edge
        return carry

    lax.fori_loop(0, fields, clear, 0)
    copy.wait()
    move(box, GHOST + radial, 0)
    build(1)
    move(box, GHOST, GHOST + cells)

    def first(r, carry):
        for t in range(wide // 8):
            row = PAD + 8 * t
            centre, rate = tile_rates(box, r, row)
            for f in range(8):
                one[f, r, row : row + 8, :] = centre[f] + time_step * rate[f]
        return carry

    lax.fori_loop(GHOST, GHOST + cells, first, 0)
    build(2)
    move(one, GHOST + radial - radial * side, (GHOST + cells) * side)

    def second(r, carry):
        at = GHOST + radial * side + r
        for t in range(out.shape[2] // 8):
            row = PAD + 2 * GHOST + 8 * t
            centre, rate = tile_rates(one, at, row)
            for f in range(8):
                start = box[f, at, row : row + 8, :]
                out[f, r, 8 * t : 8 * t + 8, :] = 0.5 * start + 0.5 * (centre[f] + time_step * rate[f])
        return carry

    lax.fori_loop(0, radial, second, 0)


def compute(side, rows, whole):
    fields, cells, wide, length = whole.shape
    padded = (fields, cells + 2 * GHOST, wide + 2 * PAD, length)
    return pl.pallas_call(
        compute_kernel,
        out_shape=jax.ShapeDtypeStruct((fields, cells // 2, wide - 4 * GHOST, length), jnp.float32),
        in_specs=[
            pl.BlockSpec(memory_space=pltpu.SMEM),
            pl.BlockSpec(memory_space=pltpu.VMEM),
            pl.BlockSpec(memory_space=pl.ANY),
        ],
        out_specs=pl.BlockSpec(memory_space=pltpu.VMEM),
        scratch_shapes=[
            pltpu.VMEM(padded, jnp.float32),
            pltpu.VMEM(padded, jnp.float32),
            pltpu.VMEM((128, length), jnp.float32),
            pltpu.VMEM((length, length), jnp.bfloat16),
            pltpu.VMEM((length, length), jnp.bfloat16),
            pltpu.SemaphoreType.DMA,
        ],
        compiler_params=pltpu.CompilerParams(vmem_limit_bytes=58 * 1024 * 1024),
        name="sections",
    )(side, rows, whole)


def remap(cells, matrix):
    return lax.dot_general(
        cells,
        matrix,
        (((cells.ndim - 1,), (0,)), ((), ())),
        precision=lax.Precision.HIGH,
        preferred_element_type=jnp.float32,
    )


def rates(left, cells, right):
    radial, vertical = cells.shape[1], cells.shape[2] - 2 * GHOST
    inner = cells[:, :, GHOST:-GHOST]
    padded = jnp.concatenate([left, inner, right], axis=1)

    def at(f, dim, step):
        if dim == 0:
            return padded[f, GHOST + step : GHOST + step + radial]
        if dim == 2:
            return cells[f, :, GHOST + step : GHOST + step + vertical]
        return jnp.roll(inner[f], -step, axis=-1)

    def d(f, dim):
        return (8.0 * (at(f, dim, 1) - at(f, dim, -1)) - (at(f, dim, 2) - at(f, dim, -2))) / 12.0

    def second(f, dim):
        return (
            16.0 * (at(f, dim, 1) + at(f, dim, -1))
            - (at(f, dim, 2) + at(f, dim, -2))
            - 30.0 * inner[f]
        ) / 12.0

    def lap(f):
        return second(f, 0) + second(f, 1) + second(f, 2)

    return jnp.stack([
        -(d(1, 0) + d(2, 1) + d(3, 2)),
        -sound_sq * d(0, 0) + guide_field * (d(4, 2) - d(6, 0)) + 2.0 * rotation * inner[2] + viscosity * lap(1),
        -sound_sq * d(0, 1) + guide_field * (d(5, 2) - d(6, 1)) - (2.0 - shear_rate) * rotation * inner[1] + viscosity * lap(2),
        -sound_sq * d(0, 2) + viscosity * lap(3),
        guide_field * d(1, 2) - d(7, 0) + resistivity * lap(4),
        guide_field * d(2, 2) - shear_rate * rotation * inner[4] - d(7, 1) + resistivity * lap(5),
        -guide_field * (d(1, 0) + d(2, 1)) - d(7, 2) + resistivity * lap(6),
        -clean_sq * (d(4, 0) + d(5, 1) + d(6, 2)) - inner[7] / damping_time,
    ])


def around(x, axis, width, dim):
    devices, length = lax.axis_size(axis), x.shape[dim]
    up = [(i, (i + 1) % devices) for i in range(devices)]
    down = [(j, i) for i, j in up]
    before = lax.ppermute(lax.slice_in_dim(x, length - width, length, axis=dim), axis, up)
    after = lax.ppermute(lax.slice_in_dim(x, 0, width, axis=dim), axis, down)
    return before, after


def body(box_state, shear_cells, shear_fraction):
    fields, radial, azimuth, vertical = box_state.shape
    gx, gy = lax.axis_size("gx"), lax.axis_size("gy")
    length, part, wide = gy * azimuth, vertical // gy, 2 * GHOST
    at_left = lax.axis_index("gx") == 0
    at_right = lax.axis_index("gx") == gx - 1
    plus, minus = jnp.int32(1), jnp.int32(-1)

    turned = jnp.transpose(box_state, (0, 1, 3, 2))
    before, after = around(turned, "gz", wide, 2)
    turned = jnp.concatenate([before, turned, after], axis=2)
    sign = jnp.where(at_left, plus, minus)

    if gx == 2 and radial == GHOST and part % 8 == 0 and azimuth % 128 == 0:
        rows = jnp.stack([
            first_rows(8, length, shear_cells[s], shear_fraction[s], way)
            for s, way in ((0, plus), (0, minus), (1, sign))
        ])
        whole = spread(turned, gy, part + 2 * wide)
        two = compute(lax.axis_index("gx").reshape(1), rows, whole)
        return jnp.transpose(gather(two, gy), (0, 1, 3, 2))

    chunks = jnp.stack([turned[:, :, part * i : part * (i + 1) + 2 * wide] for i in range(gy)])
    landed = lax.all_to_all(chunks, "gy", split_axis=0, concat_axis=0)
    own = jnp.concatenate([landed[i] for i in range(gy)], axis=-1)

    edge = circulant(length, shear_cells[1], shear_fraction[1], sign)

    def cut(x, width):
        return x[:, :, width:-width]

    def sides(x, matrix):
        before, after = around(x, "gx", GHOST, 1)
        moved = remap(jnp.where(at_left, before, after), matrix)
        return jnp.where(at_left, moved, before), jnp.where(at_right, moved, after)

    first = circulant(length, shear_cells[0], shear_fraction[0], sign)
    raw = cut(own, GHOST)
    left, right = sides(raw, first)
    mine = raw + time_step * rates(left, own, right)
    left, right = sides(cut(mine, GHOST), edge)
    two = 0.5 * cut(own, wide) + 0.5 * (cut(mine, GHOST) + time_step * rates(left, mine, right))

    pieces = jnp.stack([two[..., azimuth * i : azimuth * (i + 1)] for i in range(gy)])
    back = lax.all_to_all(pieces, "gy", split_axis=0, concat_axis=0)
    joined = jnp.concatenate([back[i] for i in range(gy)], axis=2)
    return jnp.transpose(joined, (0, 1, 3, 2))


def solution(mesh):
    return jax.shard_map(
        body,
        mesh=mesh,
        in_specs=(P(None, "gx", ("runs", "gy"), "gz"), P("runs"), P("runs")),
        out_specs=P(None, "gx", ("runs", "gy"), "gz"),
        check_vma=False,
    )
```

```python
import functools
import math

import jax
import jax.numpy as jnp
from jax import lax
from jax.experimental import pallas as pl
from jax.experimental.pallas import tpu as pltpu
from jax.sharding import PartitionSpec as P

GHOST = 2

time_step = 0.25
sound_sq = 1.0
guide_field = 0.8
rotation = 1.0
shear_rate = 1.5
viscosity = 0.15
resistivity = 0.15
clean_sq = 1.0
damping_time = 2.0


MESH = pl.DeviceIdType.MESH
PAD = 8


def first_rows(rows, length, whole_cells, fraction, sign):
    j = lax.broadcasted_iota(jnp.int32, (rows, length), 1)
    m = lax.broadcasted_iota(jnp.int32, (rows, length), 0)
    q = jnp.mod(j - m + sign * whole_cells + length // 2, length) - length // 2
    x = q.astype(jnp.float32) + sign.astype(jnp.float32) * fraction
    parity = (1 - 2 * jnp.bitwise_and(q, 1)).astype(jnp.float32) * sign.astype(jnp.float32)
    sine = jnp.sin(math.pi * jnp.minimum(fraction, 1.0 - fraction))
    angle = (math.pi / length) * x
    near = jnp.abs(x) < 1e-5
    h = parity * (sine / length) * jnp.cos(angle) / jnp.where(near, 1.0, jnp.sin(angle))
    return jnp.where(near, 1.0, h)


def circulant(length, whole_cells, fraction, sign):
    rows = math.gcd(length, 128)
    block = first_rows(rows, length, whole_cells, fraction, sign)
    return jnp.concatenate(
        [jnp.roll(block, rows * b, axis=1) for b in range(length // rows)], axis=0
    )


def tile_rates(ref, r, row):
    length = ref.shape[3]

    def load(f, dr, dv):
        return ref[f, r + dr, pl.ds(row + dv, 8), :]

    centre, diff, one, two = [], [], [], []
    for f in range(8):
        c = load(f, 0, 0)
        near = [
            (load(f, 1, 0), load(f, -1, 0), load(f, 2, 0), load(f, -2, 0)),
            tuple(pltpu.roll(c, s % length, axis=1) for s in (-1, 1, -2, 2)),
            (load(f, 0, 1), load(f, 0, -1), load(f, 0, 2), load(f, 0, -2)),
        ]
        centre.append(c)
        diff.append([(2.0 / 3.0) * (n[0] - n[1]) - (1.0 / 12.0) * (n[2] - n[3]) for n in near])
        one.append(sum(n[0] + n[1] for n in near))
        two.append(sum(n[2] + n[3] for n in near))

    def d(f, dim):
        return diff[f][dim]

    def lap(f):
        return (4.0 / 3.0) * one[f] - (1.0 / 12.0) * two[f] - 7.5 * centre[f]

    flat = d(1, 0) + d(2, 1)
    return centre, [
        -(flat + d(3, 2)),
        -sound_sq * d(0, 0) + guide_field * (d(4, 2) - d(6, 0)) + 2.0 * rotation * centre[2] + viscosity * lap(1),
        -sound_sq * d(0, 1) + guide_field * (d(5, 2) - d(6, 1)) - (2.0 - shear_rate) * rotation * centre[1] + viscosity * lap(2),
        -sound_sq * d(0, 2) + viscosity * lap(3),
        guide_field * d(1, 2) - d(7, 0) + resistivity * lap(4),
        guide_field * d(2, 2) - shear_rate * rotation * centre[4] - d(7, 1) + resistivity * lap(5),
        -guide_field * flat - d(7, 2) + resistivity * lap(6),
        -clean_sq * (d(4, 0) + d(5, 1) + d(6, 2)) - (1.0 / damping_time) * centre[7],
    ]


def sections_kernel(gy, rows_ref, src, out, box, one, two, base, high, low,
                    z_send, z_recv, x_send, x_recv, own_sem, g_send, g_recv, g_own):
    me, x = lax.axis_index("gy"), lax.axis_index("gx")
    fields, radial, tall, azimuth = src.shape
    cells, length = 2 * radial, gy * azimuth
    wide = box.shape[2] - 2 * PAD
    part = wide - 4 * GHOST
    others = [lax.rem(me + s, gy) for s in range(gy)]
    sources = [lax.rem(me - s + gy, gy) for s in range(gy)]

    def clear(f, carry):
        edge = jnp.zeros((cells + 2 * GHOST, PAD, length), jnp.float32)
        for ref in (box, one):
            ref[f, :, :PAD, :] = edge
            ref[f, :, PAD + wide :, :] = edge
        return carry

    lax.fori_loop(0, fields, clear, 0)

    barrier = pltpu.get_barrier_semaphore()
    for s in range(1, gy):
        pl.semaphore_signal(barrier, inc=1, device_id={"gy": others[s]}, device_id_type=MESH)
    pl.semaphore_signal(barrier, inc=1, device_id={"gx": 1 - x}, device_id_type=MESH)
    pl.semaphore_wait(barrier, gy)

    def taken(p, target):
        return src.at[p, :, pl.ds(pl.multiple_of(target * part, 8), wide), :]

    def place(p, source, owner):
        return box.at[
            p,
            pl.ds(GHOST + owner * radial, radial),
            pl.ds(PAD, wide),
            pl.ds(pl.multiple_of(source * azimuth, 128), azimuth),
        ]

    def over_z(p, s):
        return pltpu.make_async_remote_copy(
            src_ref=taken(p, others[s]), dst_ref=place(p, me, x),
            send_sem=z_send.at[p, s], recv_sem=z_recv.at[p, s],
            device_id={"gy": others[s]}, device_id_type=MESH,
        )

    def z_landed(p, s):
        return pltpu.make_async_remote_copy(
            src_ref=taken(p, others[s]), dst_ref=place(p, sources[s], x),
            send_sem=z_send.at[p, s], recv_sem=z_recv.at[p, s],
            device_id={"gy": others[s]}, device_id_type=MESH,
        )

    def over_x(p, s):
        return pltpu.make_async_remote_copy(
            src_ref=taken(p, me) if s == 0 else place(p, sources[s], x),
            dst_ref=place(p, sources[s], x),
            send_sem=x_send.at[p, s], recv_sem=x_recv.at[p, s],
            device_id={"gx": 1 - x}, device_id_type=MESH,
        )

    def x_landed(p, s):
        return pltpu.make_async_remote_copy(
            src_ref=taken(p, me), dst_ref=place(p, sources[s], 1 - x),
            send_sem=x_send.at[p, s], recv_sem=x_recv.at[p, s],
            device_id={"gx": 1 - x}, device_id_type=MESH,
        )

    def kept(p):
        return pltpu.make_async_copy(taken(p, me), place(p, me, x), own_sem.at[p])

    def begin(p, carry):
        over_x(p, 0).start()
        for s in range(1, gy):
            over_z(p, s).start()
        kept(p).start()
        return carry

    lax.fori_loop(0, fields, begin, 0)

    def build(i):
        block = base.shape[0]
        for a in range(block // 8):
            base[8 * a : 8 * a + 8, :] = pltpu.roll(rows_ref[i], 8 * a, axis=1) if a else rows_ref[i]
        whole = base[...]
        coarse = whole.astype(jnp.bfloat16)
        fine = (whole - coarse.astype(jnp.float32)).astype(jnp.bfloat16)
        for b in range(length // block):
            for half, ref in ((coarse, high), (fine, low)):
                cut = length - block * b
                turned = jnp.concatenate([half[:, cut:], half[:, :cut]], axis=1) if b else half
                ref[i, block * b : block * (b + 1), :] = turned

    def move(ref, i, f, count, source, target):
        v = ref[pl.ds(f, count), pl.ds(source, GHOST), PAD : PAD + wide, :]
        v = v.reshape(count * GHOST * wide, length)
        coarse = v.astype(jnp.bfloat16)
        fine = (v - coarse.astype(jnp.float32)).astype(jnp.bfloat16)
        dot = functools.partial(jnp.dot, preferred_element_type=jnp.float32)
        moved = dot(coarse, high[i]) + dot(fine, high[i]) + dot(coarse, low[i])
        ref[pl.ds(f, count), pl.ds(target, GHOST), PAD : PAD + wide, :] = moved.reshape(
            count, GHOST, wide, length
        )

    def forward(p):
        for s in range(1, gy):
            z_landed(p, s).wait_recv()
            over_x(p, s).start()

    def finish(p):
        kept(p).wait()
        for s in range(gy):
            x_landed(p, s).wait_recv()
        move(box, 0, p, 1, GHOST + radial, 0)
        move(box, 1, p, 1, GHOST, GHOST + cells)

    build(0)
    build(1)
    forward(0)

    def piece(p, carry):
        forward(p)
        finish(p - 1)
        return carry

    build(2)
    lax.fori_loop(1, fields, piece, 0)
    finish(fields - 1)

    def sent(p, carry):
        for s in range(gy):
            over_x(p, s).wait_send()
            if s:
                over_z(p, s).wait_send()
        return carry

    lax.fori_loop(0, fields, sent, 0)

    def first(r, carry):
        for t in range(wide // 8):
            row = PAD + 8 * t
            centre, rate = tile_rates(box, r, row)
            for f in range(8):
                one[f, r, row : row + 8, :] = centre[f] + time_step * rate[f]
        return carry

    lax.fori_loop(GHOST, GHOST + cells, first, 0)

    def edge(k, carry):
        move(one, 2, 4 * k, 4, GHOST + radial - radial * x, (GHOST + cells) * x)
        return carry

    lax.fori_loop(0, fields // 4, edge, 0)

    copies = []
    for t in range(part // 8):
        row = PAD + 2 * GHOST + 8 * t

        def second(r, carry):
            at = GHOST + radial * x + r
            centre, rate = tile_rates(one, at, row)
            for f in range(8):
                start = box[f, at, row : row + 8, :]
                two[f, r, 8 * t : 8 * t + 8, :] = 0.5 * start + 0.5 * (centre[f] + time_step * rate[f])
            return carry

        lax.fori_loop(0, radial, second, 0)

        def tile(target):
            return two.at[:, :, pl.ds(8 * t, 8), pl.ds(pl.multiple_of(target * azimuth, 128), azimuth)]

        def home(source):
            return out.at[:, :, pl.ds(pl.multiple_of(source * part + 8 * t, 8), 8), :]

        for s in range(1, gy):
            back = pltpu.make_async_remote_copy(
                src_ref=tile(others[s]), dst_ref=home(me),
                send_sem=g_send.at[t, s], recv_sem=g_recv.at[t, s],
                device_id={"gy": others[s]}, device_id_type=MESH,
            )
            back.start()
            copies.append(back)
        own = pltpu.make_async_copy(tile(me), home(me), g_own.at[t])
        own.start()
        copies.append(own)
    for back in copies:
        back.wait()


def sections(rows, turned, gy, wide):
    fields, radial, tall, azimuth = turned.shape
    length, part = gy * azimuth, wide - 4 * GHOST
    padded = (fields, 2 * radial + 2 * GHOST, wide + 2 * PAD, length)
    dma = pltpu.SemaphoreType.DMA
    return pl.pallas_call(
        functools.partial(sections_kernel, gy),
        out_shape=jax.ShapeDtypeStruct((fields, radial, part * gy, azimuth), jnp.float32),
        in_specs=[pl.BlockSpec(memory_space=pltpu.VMEM), pl.BlockSpec(memory_space=pl.ANY)],
        out_specs=pl.BlockSpec(memory_space=pl.ANY),
        scratch_shapes=[
            pltpu.VMEM(padded, jnp.float32),
            pltpu.VMEM(padded, jnp.float32),
            pltpu.VMEM((fields, radial, part, length), jnp.float32),
            pltpu.VMEM((128, length), jnp.float32),
            pltpu.VMEM((3, length, length), jnp.bfloat16),
            pltpu.VMEM((3, length, length), jnp.bfloat16),
            dma((fields, gy)),
            dma((fields, gy)),
            dma((fields, gy)),
            dma((fields, gy)),
            dma((fields,)),
            dma((part // 8, gy)),
            dma((part // 8, gy)),
            dma((part // 8,)),
        ],
        compiler_params=pltpu.CompilerParams(
            collective_id=0, has_side_effects=True, vmem_limit_bytes=58 * 1024 * 1024
        ),
        name="sections",
    )(rows, turned)


def remap(cells, matrix):
    return lax.dot_general(
        cells,
        matrix,
        (((cells.ndim - 1,), (0,)), ((), ())),
        precision=lax.Precision.HIGH,
        preferred_element_type=jnp.float32,
    )


def rates(left, cells, right):
    radial, vertical = cells.shape[1], cells.shape[2] - 2 * GHOST
    inner = cells[:, :, GHOST:-GHOST]
    padded = jnp.concatenate([left, inner, right], axis=1)

    def at(f, dim, step):
        if dim == 0:
            return padded[f, GHOST + step : GHOST + step + radial]
        if dim == 2:
            return cells[f, :, GHOST + step : GHOST + step + vertical]
        return jnp.roll(inner[f], -step, axis=-1)

    def d(f, dim):
        return (8.0 * (at(f, dim, 1) - at(f, dim, -1)) - (at(f, dim, 2) - at(f, dim, -2))) / 12.0

    def second(f, dim):
        return (
            16.0 * (at(f, dim, 1) + at(f, dim, -1))
            - (at(f, dim, 2) + at(f, dim, -2))
            - 30.0 * inner[f]
        ) / 12.0

    def lap(f):
        return second(f, 0) + second(f, 1) + second(f, 2)

    return jnp.stack([
        -(d(1, 0) + d(2, 1) + d(3, 2)),
        -sound_sq * d(0, 0) + guide_field * (d(4, 2) - d(6, 0)) + 2.0 * rotation * inner[2] + viscosity * lap(1),
        -sound_sq * d(0, 1) + guide_field * (d(5, 2) - d(6, 1)) - (2.0 - shear_rate) * rotation * inner[1] + viscosity * lap(2),
        -sound_sq * d(0, 2) + viscosity * lap(3),
        guide_field * d(1, 2) - d(7, 0) + resistivity * lap(4),
        guide_field * d(2, 2) - shear_rate * rotation * inner[4] - d(7, 1) + resistivity * lap(5),
        -guide_field * (d(1, 0) + d(2, 1)) - d(7, 2) + resistivity * lap(6),
        -clean_sq * (d(4, 0) + d(5, 1) + d(6, 2)) - inner[7] / damping_time,
    ])


def around(x, axis, width, dim):
    devices, length = lax.axis_size(axis), x.shape[dim]
    up = [(i, (i + 1) % devices) for i in range(devices)]
    down = [(j, i) for i, j in up]
    before = lax.ppermute(lax.slice_in_dim(x, length - width, length, axis=dim), axis, up)
    after = lax.ppermute(lax.slice_in_dim(x, 0, width, axis=dim), axis, down)
    return before, after


def body(box_state, shear_cells, shear_fraction):
    fields, radial, azimuth, vertical = box_state.shape
    gx, gy = lax.axis_size("gx"), lax.axis_size("gy")
    length, part, wide = gy * azimuth, vertical // gy, 2 * GHOST
    at_left = lax.axis_index("gx") == 0
    at_right = lax.axis_index("gx") == gx - 1
    plus, minus = jnp.int32(1), jnp.int32(-1)

    turned = jnp.transpose(box_state, (0, 1, 3, 2))
    before, after = around(turned, "gz", wide, 2)
    turned = jnp.concatenate([before, turned, after], axis=2)
    sign = jnp.where(at_left, plus, minus)

    if gx == 2 and radial == GHOST and part % 8 == 0 and azimuth % 128 == 0:
        rows = jnp.stack([
            first_rows(8, length, shear_cells[s], shear_fraction[s], way)
            for s, way in ((0, plus), (0, minus), (1, sign))
        ])
        joined = sections(rows, turned, gy, part + 2 * wide)
        return jnp.transpose(joined, (0, 1, 3, 2))

    chunks = jnp.stack([turned[:, :, part * i : part * (i + 1) + 2 * wide] for i in range(gy)])
    landed = lax.all_to_all(chunks, "gy", split_axis=0, concat_axis=0)
    own = jnp.concatenate([landed[i] for i in range(gy)], axis=-1)

    edge = circulant(length, shear_cells[1], shear_fraction[1], sign)

    def cut(x, width):
        return x[:, :, width:-width]

    def sides(x, matrix):
        before, after = around(x, "gx", GHOST, 1)
        moved = remap(jnp.where(at_left, before, after), matrix)
        return jnp.where(at_left, moved, before), jnp.where(at_right, moved, after)

    first = circulant(length, shear_cells[0], shear_fraction[0], sign)
    raw = cut(own, GHOST)
    left, right = sides(raw, first)
    mine = raw + time_step * rates(left, own, right)
    left, right = sides(cut(mine, GHOST), edge)
    two = 0.5 * cut(own, wide) + 0.5 * (cut(mine, GHOST) + time_step * rates(left, mine, right))

    pieces = jnp.stack([two[..., azimuth * i : azimuth * (i + 1)] for i in range(gy)])
    back = lax.all_to_all(pieces, "gy", split_axis=0, concat_axis=0)
    joined = jnp.concatenate([back[i] for i in range(gy)], axis=2)
    return jnp.transpose(joined, (0, 1, 3, 2))


def solution(mesh):
    return jax.shard_map(
        body,
        mesh=mesh,
        in_specs=(P(None, "gx", ("runs", "gy"), "gz"), P("runs"), P("runs")),
        out_specs=P(None, "gx", ("runs", "gy"), "gz"),
        check_vma=False,
    )
```

```python
import functools
import math

import jax
import jax.numpy as jnp
from jax import lax
from jax.experimental import pallas as pl
from jax.experimental.pallas import tpu as pltpu
from jax.sharding import PartitionSpec as P

GHOST = 2

time_step = 0.25
sound_sq = 1.0
guide_field = 0.8
rotation = 1.0
shear_rate = 1.5
viscosity = 0.15
resistivity = 0.15
clean_sq = 1.0
damping_time = 2.0


MESH = pl.DeviceIdType.MESH
PAD = 8


def first_rows(rows, length, whole_cells, fraction, sign):
    j = lax.broadcasted_iota(jnp.int32, (rows, length), 1)
    m = lax.broadcasted_iota(jnp.int32, (rows, length), 0)
    q = jnp.mod(j - m + sign * whole_cells + length // 2, length) - length // 2
    x = q.astype(jnp.float32) + sign.astype(jnp.float32) * fraction
    parity = (1 - 2 * jnp.bitwise_and(q, 1)).astype(jnp.float32) * sign.astype(jnp.float32)
    sine = jnp.sin(math.pi * jnp.minimum(fraction, 1.0 - fraction))
    angle = (math.pi / length) * x
    near = jnp.abs(x) < 1e-5
    h = parity * (sine / length) * jnp.cos(angle) / jnp.where(near, 1.0, jnp.sin(angle))
    return jnp.where(near, 1.0, h)


def circulant(length, whole_cells, fraction, sign):
    rows = math.gcd(length, 128)
    block = first_rows(rows, length, whole_cells, fraction, sign)
    return jnp.concatenate(
        [jnp.roll(block, rows * b, axis=1) for b in range(length // rows)], axis=0
    )


def tile_rates(ref, r, row):
    length = ref.shape[3]

    def load(f, dr, dv):
        return ref[f, r + dr, pl.ds(row + dv, 8), :]

    centre, diff, one, two = [], [], [], []
    for f in range(8):
        c = load(f, 0, 0)
        near = [
            (load(f, 1, 0), load(f, -1, 0), load(f, 2, 0), load(f, -2, 0)),
            tuple(pltpu.roll(c, s % length, axis=1) for s in (-1, 1, -2, 2)),
            (load(f, 0, 1), load(f, 0, -1), load(f, 0, 2), load(f, 0, -2)),
        ]
        centre.append(c)
        diff.append([(2.0 / 3.0) * (n[0] - n[1]) - (1.0 / 12.0) * (n[2] - n[3]) for n in near])
        one.append(sum(n[0] + n[1] for n in near))
        two.append(sum(n[2] + n[3] for n in near))

    def d(f, dim):
        return diff[f][dim]

    def lap(f):
        return (4.0 / 3.0) * one[f] - (1.0 / 12.0) * two[f] - 7.5 * centre[f]

    flat = d(1, 0) + d(2, 1)
    return centre, [
        -(flat + d(3, 2)),
        -sound_sq * d(0, 0) + guide_field * (d(4, 2) - d(6, 0)) + 2.0 * rotation * centre[2] + viscosity * lap(1),
        -sound_sq * d(0, 1) + guide_field * (d(5, 2) - d(6, 1)) - (2.0 - shear_rate) * rotation * centre[1] + viscosity * lap(2),
        -sound_sq * d(0, 2) + viscosity * lap(3),
        guide_field * d(1, 2) - d(7, 0) + resistivity * lap(4),
        guide_field * d(2, 2) - shear_rate * rotation * centre[4] - d(7, 1) + resistivity * lap(5),
        -guide_field * flat - d(7, 2) + resistivity * lap(6),
        -clean_sq * (d(4, 0) + d(5, 1) + d(6, 2)) - (1.0 / damping_time) * centre[7],
    ]


def sections_kernel(gy, rows_ref, state, out, src, edge_out, edge_in, box, one, two, base, high, low,
                    z_send, z_recv, x_send, x_recv, own_sem, g_send, g_recv, g_own, e_sem):
    me, x = lax.axis_index("gy"), lax.axis_index("gx")
    fields, radial, tall, azimuth = src.shape
    cells, length = 2 * radial, gy * azimuth
    wide = box.shape[2] - 2 * PAD
    part = wide - 4 * GHOST
    others = [lax.rem(me + s, gy) for s in range(gy)]
    sources = [lax.rem(me - s + gy, gy) for s in range(gy)]

    def clear(f, carry):
        edge = jnp.zeros((cells + 2 * GHOST, PAD, length), jnp.float32)
        for ref in (box, one):
            ref[f, :, :PAD, :] = edge
            ref[f, :, PAD + wide :, :] = edge
        return carry

    lax.fori_loop(0, fields, clear, 0)
    margin = 2 * GHOST
    vertical = tall - 2 * margin

    def turn(f, carry):
        for r in range(radial):
            v = jnp.transpose(state[f, r])
            src[f, r, margin : margin + vertical, :] = v
            edge_out[f, r, :margin, :] = v[vertical - margin :]
            edge_out[f, r, margin:, :] = v[:margin]
        return carry

    lax.fori_loop(0, fields, turn, 0)

    barrier = pltpu.get_barrier_semaphore()
    for s in range(1, gy):
        pl.semaphore_signal(barrier, inc=1, device_id={"gy": others[s]}, device_id_type=MESH)
    pl.semaphore_signal(barrier, inc=1, device_id={"gx": 1 - x}, device_id_type=MESH)
    beside = {"gz": 1 - lax.axis_index("gz")}
    pl.semaphore_signal(barrier, inc=1, device_id=beside, device_id_type=MESH)
    pl.semaphore_wait(barrier, gy + 1)
    swap = pltpu.make_async_remote_copy(
        src_ref=edge_out, dst_ref=edge_in, send_sem=e_sem.at[0], recv_sem=e_sem.at[1],
        device_id=beside, device_id_type=MESH,
    )
    swap.start()
    swap.wait()
    src[:, :, :margin, :] = edge_in[:, :, :margin, :]
    src[:, :, margin + vertical :, :] = edge_in[:, :, margin:, :]

    def taken(p, target):
        return src.at[p, :, pl.ds(pl.multiple_of(target * part, 8), wide), :]

    def place(p, source, owner):
        return box.at[
            p,
            pl.ds(GHOST + owner * radial, radial),
            pl.ds(PAD, wide),
            pl.ds(pl.multiple_of(source * azimuth, 128), azimuth),
        ]

    def over_z(p, s):
        return pltpu.make_async_remote_copy(
            src_ref=taken(p, others[s]), dst_ref=place(p, me, x),
            send_sem=z_send.at[p, s], recv_sem=z_recv.at[p, s],
            device_id={"gy": others[s]}, device_id_type=MESH,
        )

    def z_landed(p, s):
        return pltpu.make_async_remote_copy(
            src_ref=taken(p, others[s]), dst_ref=place(p, sources[s], x),
            send_sem=z_send.at[p, s], recv_sem=z_recv.at[p, s],
            device_id={"gy": others[s]}, device_id_type=MESH,
        )

    def over_x(p, s):
        return pltpu.make_async_remote_copy(
            src_ref=taken(p, me) if s == 0 else place(p, sources[s], x),
            dst_ref=place(p, sources[s], x),
            send_sem=x_send.at[p, s], recv_sem=x_recv.at[p, s],
            device_id={"gx": 1 - x}, device_id_type=MESH,
        )

    def x_landed(p, s):
        return pltpu.make_async_remote_copy(
            src_ref=taken(p, me), dst_ref=place(p, sources[s], 1 - x),
            send_sem=x_send.at[p, s], recv_sem=x_recv.at[p, s],
            device_id={"gx": 1 - x}, device_id_type=MESH,
        )

    def kept(p):
        return pltpu.make_async_copy(taken(p, me), place(p, me, x), own_sem.at[p])

    def begin(p, carry):
        over_x(p, 0).start()
        for s in range(1, gy):
            over_z(p, s).start()
        kept(p).start()
        return carry

    lax.fori_loop(0, fields, begin, 0)

    def build(i):
        block = base.shape[0]
        for a in range(block // 8):
            base[8 * a : 8 * a + 8, :] = pltpu.roll(rows_ref[i], 8 * a, axis=1) if a else rows_ref[i]
        whole = base[...]
        coarse = whole.astype(jnp.bfloat16)
        fine = (whole - coarse.astype(jnp.float32)).astype(jnp.bfloat16)
        for b in range(length // block):
            for half, ref in ((coarse, high), (fine, low)):
                cut = length - block * b
                turned = jnp.concatenate([half[:, cut:], half[:, :cut]], axis=1) if b else half
                ref[i, block * b : block * (b + 1), :] = turned

    def move(ref, i, f, count, source, target):
        v = ref[pl.ds(f, count), pl.ds(source, GHOST), PAD : PAD + wide, :]
        v = v.reshape(count * GHOST * wide, length)
        coarse = v.astype(jnp.bfloat16)
        fine = (v - coarse.astype(jnp.float32)).astype(jnp.bfloat16)
        dot = functools.partial(jnp.dot, preferred_element_type=jnp.float32)
        moved = dot(coarse, high[i]) + dot(fine, high[i]) + dot(coarse, low[i])
        ref[pl.ds(f, count), pl.ds(target, GHOST), PAD : PAD + wide, :] = moved.reshape(
            count, GHOST, wide, length
        )

    def forward(p):
        for s in range(1, gy):
            z_landed(p, s).wait_recv()
            over_x(p, s).start()

    def finish(p):
        kept(p).wait()
        for s in range(gy):
            x_landed(p, s).wait_recv()
        move(box, 0, p, 1, GHOST + radial, 0)
        move(box, 1, p, 1, GHOST, GHOST + cells)

    build(0)
    build(1)
    forward(0)

    def piece(p, carry):
        forward(p)
        finish(p - 1)
        return carry

    build(2)
    lax.fori_loop(1, fields, piece, 0)
    finish(fields - 1)

    def sent(p, carry):
        for s in range(gy):
            over_x(p, s).wait_send()
            if s:
                over_z(p, s).wait_send()
        return carry

    lax.fori_loop(0, fields, sent, 0)

    def first(r, carry):
        for t in range(wide // 8):
            row = PAD + 8 * t
            centre, rate = tile_rates(box, r, row)
            for f in range(8):
                one[f, r, row : row + 8, :] = centre[f] + time_step * rate[f]
        return carry

    lax.fori_loop(GHOST, GHOST + cells, first, 0)

    def edge(k, carry):
        move(one, 2, 4 * k, 4, GHOST + radial - radial * x, (GHOST + cells) * x)
        return carry

    lax.fori_loop(0, fields // 4, edge, 0)

    copies = []
    for t in range(part // 8):
        row = PAD + 2 * GHOST + 8 * t

        def second(r, carry):
            at = GHOST + radial * x + r
            centre, rate = tile_rates(one, at, row)
            for f in range(8):
                start = box[f, at, row : row + 8, :]
                two[f, r, 8 * t : 8 * t + 8, :] = 0.5 * start + 0.5 * (centre[f] + time_step * rate[f])
            return carry

        lax.fori_loop(0, radial, second, 0)

        def tile(target):
            return two.at[:, :, pl.ds(8 * t, 8), pl.ds(pl.multiple_of(target * azimuth, 128), azimuth)]

        def home(source):
            return out.at[:, :, pl.ds(pl.multiple_of(source * part + 8 * t, 8), 8), :]

        for s in range(1, gy):
            back = pltpu.make_async_remote_copy(
                src_ref=tile(others[s]), dst_ref=home(me),
                send_sem=g_send.at[t, s], recv_sem=g_recv.at[t, s],
                device_id={"gy": others[s]}, device_id_type=MESH,
            )
            back.start()
            copies.append(back)
        own = pltpu.make_async_copy(tile(me), home(me), g_own.at[t])
        own.start()
        copies.append(own)
    for back in copies:
        back.wait()


def sections(rows, state, gy, wide):
    fields, radial, azimuth, vertical = state.shape
    tall = vertical + 4 * GHOST
    length, part = gy * azimuth, wide - 4 * GHOST
    padded = (fields, 2 * radial + 2 * GHOST, wide + 2 * PAD, length)
    dma = pltpu.SemaphoreType.DMA
    return pl.pallas_call(
        functools.partial(sections_kernel, gy),
        out_shape=jax.ShapeDtypeStruct((fields, radial, part * gy, azimuth), jnp.float32),
        in_specs=[pl.BlockSpec(memory_space=pltpu.VMEM)] * 2,
        out_specs=pl.BlockSpec(memory_space=pl.ANY),
        scratch_shapes=[
            pltpu.VMEM((fields, radial, tall, azimuth), jnp.float32),
            pltpu.VMEM((fields, radial, 4 * GHOST, azimuth), jnp.float32),
            pltpu.VMEM((fields, radial, 4 * GHOST, azimuth), jnp.float32),
            pltpu.VMEM(padded, jnp.float32),
            pltpu.VMEM(padded, jnp.float32),
            pltpu.VMEM((fields, radial, part, length), jnp.float32),
            pltpu.VMEM((128, length), jnp.float32),
            pltpu.VMEM((3, length, length), jnp.bfloat16),
            pltpu.VMEM((3, length, length), jnp.bfloat16),
            dma((fields, gy)),
            dma((fields, gy)),
            dma((fields, gy)),
            dma((fields, gy)),
            dma((fields,)),
            dma((part // 8, gy)),
            dma((part // 8, gy)),
            dma((part // 8,)),
            dma((2,)),
        ],
        compiler_params=pltpu.CompilerParams(
            collective_id=0, has_side_effects=True, vmem_limit_bytes=58 * 1024 * 1024
        ),
        name="sections",
    )(rows, state)


def remap(cells, matrix):
    return lax.dot_general(
        cells,
        matrix,
        (((cells.ndim - 1,), (0,)), ((), ())),
        precision=lax.Precision.HIGH,
        preferred_element_type=jnp.float32,
    )


def rates(left, cells, right):
    radial, vertical = cells.shape[1], cells.shape[2] - 2 * GHOST
    inner = cells[:, :, GHOST:-GHOST]
    padded = jnp.concatenate([left, inner, right], axis=1)

    def at(f, dim, step):
        if dim == 0:
            return padded[f, GHOST + step : GHOST + step + radial]
        if dim == 2:
            return cells[f, :, GHOST + step : GHOST + step + vertical]
        return jnp.roll(inner[f], -step, axis=-1)

    def d(f, dim):
        return (8.0 * (at(f, dim, 1) - at(f, dim, -1)) - (at(f, dim, 2) - at(f, dim, -2))) / 12.0

    def second(f, dim):
        return (
            16.0 * (at(f, dim, 1) + at(f, dim, -1))
            - (at(f, dim, 2) + at(f, dim, -2))
            - 30.0 * inner[f]
        ) / 12.0

    def lap(f):
        return second(f, 0) + second(f, 1) + second(f, 2)

    return jnp.stack([
        -(d(1, 0) + d(2, 1) + d(3, 2)),
        -sound_sq * d(0, 0) + guide_field * (d(4, 2) - d(6, 0)) + 2.0 * rotation * inner[2] + viscosity * lap(1),
        -sound_sq * d(0, 1) + guide_field * (d(5, 2) - d(6, 1)) - (2.0 - shear_rate) * rotation * inner[1] + viscosity * lap(2),
        -sound_sq * d(0, 2) + viscosity * lap(3),
        guide_field * d(1, 2) - d(7, 0) + resistivity * lap(4),
        guide_field * d(2, 2) - shear_rate * rotation * inner[4] - d(7, 1) + resistivity * lap(5),
        -guide_field * (d(1, 0) + d(2, 1)) - d(7, 2) + resistivity * lap(6),
        -clean_sq * (d(4, 0) + d(5, 1) + d(6, 2)) - inner[7] / damping_time,
    ])


def around(x, axis, width, dim):
    devices, length = lax.axis_size(axis), x.shape[dim]
    up = [(i, (i + 1) % devices) for i in range(devices)]
    down = [(j, i) for i, j in up]
    before = lax.ppermute(lax.slice_in_dim(x, length - width, length, axis=dim), axis, up)
    after = lax.ppermute(lax.slice_in_dim(x, 0, width, axis=dim), axis, down)
    return before, after


def body(box_state, shear_cells, shear_fraction):
    fields, radial, azimuth, vertical = box_state.shape
    gx, gy = lax.axis_size("gx"), lax.axis_size("gy")
    length, part, wide = gy * azimuth, vertical // gy, 2 * GHOST
    at_left = lax.axis_index("gx") == 0
    at_right = lax.axis_index("gx") == gx - 1
    plus, minus = jnp.int32(1), jnp.int32(-1)

    sign = jnp.where(at_left, plus, minus)

    if gx == 2 and lax.axis_size("gz") == 2 and radial == GHOST and part % 8 == 0 and azimuth % 128 == 0:
        rows = jnp.stack([
            first_rows(8, length, shear_cells[s], shear_fraction[s], way)
            for s, way in ((0, plus), (0, minus), (1, sign))
        ])
        joined = sections(rows, box_state, gy, part + 2 * wide)
        return jnp.transpose(joined, (0, 1, 3, 2))

    turned = jnp.transpose(box_state, (0, 1, 3, 2))
    before, after = around(turned, "gz", wide, 2)
    turned = jnp.concatenate([before, turned, after], axis=2)
    chunks = jnp.stack([turned[:, :, part * i : part * (i + 1) + 2 * wide] for i in range(gy)])
    landed = lax.all_to_all(chunks, "gy", split_axis=0, concat_axis=0)
    own = jnp.concatenate([landed[i] for i in range(gy)], axis=-1)

    edge = circulant(length, shear_cells[1], shear_fraction[1], sign)

    def cut(x, width):
        return x[:, :, width:-width]

    def sides(x, matrix):
        before, after = around(x, "gx", GHOST, 1)
        moved = remap(jnp.where(at_left, before, after), matrix)
        return jnp.where(at_left, moved, before), jnp.where(at_right, moved, after)

    first = circulant(length, shear_cells[0], shear_fraction[0], sign)
    raw = cut(own, GHOST)
    left, right = sides(raw, first)
    mine = raw + time_step * rates(left, own, right)
    left, right = sides(cut(mine, GHOST), edge)
    two = 0.5 * cut(own, wide) + 0.5 * (cut(mine, GHOST) + time_step * rates(left, mine, right))

    pieces = jnp.stack([two[..., azimuth * i : azimuth * (i + 1)] for i in range(gy)])
    back = lax.all_to_all(pieces, "gy", split_axis=0, concat_axis=0)
    joined = jnp.concatenate([back[i] for i in range(gy)], axis=2)
    return jnp.transpose(joined, (0, 1, 3, 2))


def solution(mesh):
    return jax.shard_map(
        body,
        mesh=mesh,
        in_specs=(P(None, "gx", ("runs", "gy"), "gz"), P("runs"), P("runs")),
        out_specs=P(None, "gx", ("runs", "gy"), "gz"),
        check_vma=False,
    )
```
